32 devices in a mesh: groups: 2 (over y), dp: 4 (over z), mp: 2 (over x), role: 2 (over core).
Axes of the slice: x: 2, y: 2, z: 4, core: 2. Of those that a mesh axis runs over, the one named last changes fastest.
Arguments:
- train_x: bfloat16 [4096, 8192], P(('groups', 'dp', 'role'), 'mp'), parts along dimension 0, may hold values from -6 to 6
- train_cot: bfloat16 [4096, 4096], P(('groups', 'dp', 'role'), 'mp'), parts along dimension 0, may hold values from -6 to 6
- tenant_of_block: int32 [32], P(('groups', 'dp', 'role')), parts along dimension 0, may hold values from 0 to 7
- down_factors: float32 [512, 8192], P(('groups', 'dp', 'role'), 'mp'), parts along dimension 0, may hold values from -0.0625 to 0.0625
- up_factors: float32 [512, 4096], P(('groups', 'dp', 'role'), 'mp'), parts along dimension 0, may hold values from -1 to 1
- down_mean_moment: float32 [512, 8192], P(('groups', 'dp', 'role'), 'mp'), parts along dimension 0, may hold values from -120 to 120
- down_square_moment: float32 [512, 8192], P(('groups', 'dp', 'role'), 'mp'), parts along dimension 0, may hold values from 100 to 10000
- up_mean_moment: float32 [512, 4096], P(('groups', 'dp', 'role'), 'mp'), parts along dimension 0, may hold values from -120 to 120
- up_square_moment: float32 [512, 4096], P(('groups', 'dp', 'role'), 'mp'), parts along dimension 0, may hold values from 100 to 10000
- base_weight: bfloat16 [8192, 4096], P('mp', ('dp', 'role')), may hold values from -0.0625 to 0.0625
- base_scale: bfloat16 [128, 4096], P('mp', ('dp', 'role')), may hold values from 0.5 to 2
- row_hidden: bfloat16 [32, 8192], P(('groups', 'dp', 'role')), parts along dimension 0, may hold values from -6 to 6
- row_tenant: int32 [32], P(('groups', 'dp', 'role')), parts along dimension 0, may hold values from 0 to 7
- cache_len: int32 [32], P(('groups', 'dp', 'role')), parts along dimension 0, may hold values from 1 to 1024, as said below
- kv_cache: bfloat16 [32, 8, 1024, 256], P(('groups', 'dp', 'role'), 'mp'), parts along dimension 0, may hold values from -2000 to 2000
- new_kv: bfloat16 [32, 8, 256], P(('groups', 'dp', 'role'), 'mp'), parts along dimension 0, may hold values from -6 to 6
Outputs:
- down_direction: float32 [512, 8192], P(('groups', 'dp', 'role'), 'mp'), parts along dimension 0
- up_direction: float32 [512, 4096], P(('groups', 'dp', 'role'), 'mp'), parts along dimension 0
- training_input_gradient: bfloat16 [4096, 8192], P(('groups', 'dp', 'role'), 'mp'), parts along dimension 0
- attended: bfloat16 [32, 4096], P(('groups', 'dp', 'role'), 'mp'), parts along dimension 0
The draws below stay inside these ranges and needn't reach their ends.
There are 2 independent parts, one for each index of `groups`. The reference program is written for one: setup_inputs(seed, part) draws one part's arguments, and reference() takes and returns one part's arrays. A program takes and returns all parts, laid end to end along the dimension named above; an argument that names none is the same for every part. Nothing has to cross between parts.
Inputs may be any that keep to these rules, and one draw needn't show every extreme that they name: `cache_len`: some row has exactly 1024 valid positions.
All inputs are finite; a program needn't handle non-finite values.
Results may differ from the reference program's by a relative error of at most 0.007.
Values may be sent and summed in bfloat16 or wider, within the bound.
No kernel may reach another device: no remote copies, remote signals or barrier semaphores. Data moves between devices by JAX's collectives and lax.ppermute only.
A program may use at most 192 MiB of HBM per device.

```python
import math
import jax
import jax.numpy as jnp
import numpy as np
from jax import lax

MODEL_WIDTH = 8192
KV_HEADS = 8
HEAD_DIM = 128
ADAPTER_RANK = 32
TENANT_COUNT = 8
GROUP = 64
BLOCK = 128
CACHE = 1024
QUERY_WIDTH = 4096
TRAIN_TOKENS = 2048
ROWS = 16


def draw_cache_len(key, part):
    key = jax.random.fold_in(key, 7)
    first_key, second_key = jax.random.split(key)
    lengths = jax.random.randint(first_key, (ROWS,), 1, CACHE + 1)
    marked = jax.random.randint(second_key, (), 0, ROWS)
    return jnp.where(jnp.arange(ROWS) == marked, CACHE, lengths).astype(jnp.int32)


def draw_kv_cache(key, part):
    key = jax.random.fold_in(key, 11)
    noise_key = jax.random.fold_in(key, 0)
    shape = (ROWS, KV_HEADS, CACHE, 2 * HEAD_DIM)
    entries = jnp.clip(jax.random.normal(noise_key, shape, jnp.float32), -6.0, 6.0)
    return entries.astype(jnp.bfloat16)


def with_ends(drawn, key, least, largest):
    longest = drawn.shape.index(max(drawn.shape))
    spots = []
    for shift in (0, 1):
        where = [jax.random.randint(jax.random.fold_in(key, axis), (), 0, length) for axis, length in enumerate(drawn.shape)]
        where[longest] = (where[longest] + shift) % drawn.shape[longest]
        spots.append(tuple(where))
    return drawn.at[spots[0]].set(least).at[spots[1]].set(largest)


def levels(stream_key, extent, shards, smallest, top_value):
    loudness, own = 1.0, jax.random.fold_in(stream_key, 6)
    for dim, blocks in shards:
        steps = jnp.exp(jax.random.uniform(jax.random.fold_in(own, dim), (blocks,), jnp.float32, smallest / len(shards), top_value / len(shards)))
        loudness = loudness * jnp.repeat(steps, extent[dim] // blocks).reshape([-1 if axis == dim else 1 for axis in range(len(extent))])
    return loudness


def rank_table(count, lean):
    portions = [(1 << 20) // math.isqrt(rank ** lean) + 1 for rank in range(1, count + 1)]
    width = 1 + sum(portions) // (1 << 30)
    return np.cumsum(np.array([max(1, weight // width) for weight in portions]))


def skewed_ids(key, dims, count, lean):
    listing = rank_table(count, lean)
    lot = jax.random.randint(jax.random.fold_in(key, 1), dims, 0, int(listing[count - 1]))
    rank = jnp.searchsorted(jnp.asarray(listing, jnp.int32), lot, side="right")
    return jax.random.permutation(jax.random.fold_in(key, 2), count)[rank].astype(jnp.int32)


def centred(key, shape, deviation, reach, pieces=(), held_as=jnp.bfloat16):
    factor_of = levels(key, shape, pieces, -0.22, 0.18) if pieces else 1.0
    values = jax.random.normal(key, shape, jnp.float32) * deviation * factor_of
    return jnp.minimum(jnp.maximum(values, -reach), reach).astype(held_as)


def setup_inputs(seed: int = 0, part: int = 0) -> dict:
    seeds = jax.random.split(jax.random.key(seed), 17)
    own_keys = jax.random.split(jax.random.fold_in(seeds[16], part), 17)
    train_x = centred(own_keys[0], (TRAIN_TOKENS, MODEL_WIDTH), 1.0, 6.0, ((0, 8), (1, 2)))
    train_cot = centred(own_keys[1], (TRAIN_TOKENS, QUERY_WIDTH), 1.0, 6.0, ((0, 8), (1, 2)))
    tenant_of_block = with_ends(jax.random.randint(own_keys[2], (TRAIN_TOKENS // BLOCK,), 0, TENANT_COUNT), jax.random.fold_in(own_keys[2], 1), 0, TENANT_COUNT - 1).astype(jnp.int32)
    down_factors = centred(own_keys[3], (TENANT_COUNT * ADAPTER_RANK, MODEL_WIDTH), MODEL_WIDTH ** -0.5, 0.0625, ((0, 8), (1, 2)), jnp.float32)
    up_factors = centred(own_keys[4], (TENANT_COUNT * ADAPTER_RANK, QUERY_WIDTH), ADAPTER_RANK ** -0.5, 1.0, ((0, 8), (1, 2)), jnp.float32)
    down_mean_moment = centred(own_keys[5], (TENANT_COUNT * ADAPTER_RANK, MODEL_WIDTH), 20.0, 120.0, ((0, 8), (1, 2)), jnp.float32)
    down_square_moment = jnp.clip(jnp.exp(math.log(10000.0) - 4.6051702 * jax.random.uniform(own_keys[6], (TENANT_COUNT * ADAPTER_RANK, MODEL_WIDTH), jnp.float32) ** levels(own_keys[6], (TENANT_COUNT * ADAPTER_RANK, MODEL_WIDTH), ((0, 8), (1, 2)), -0.2, 0.2)), 100.0, 10000.0)
    up_mean_moment = centred(own_keys[7], (TENANT_COUNT * ADAPTER_RANK, QUERY_WIDTH), 20.0, 120.0, ((0, 8), (1, 2)), jnp.float32)
    up_square_moment = jnp.clip(jnp.exp(math.log(10000.0) - 4.6051702 * jax.random.uniform(own_keys[8], (TENANT_COUNT * ADAPTER_RANK, QUERY_WIDTH), jnp.float32) ** levels(own_keys[8], (TENANT_COUNT * ADAPTER_RANK, QUERY_WIDTH), ((0, 8), (1, 2)), -0.2, 0.2)), 100.0, 10000.0)
    base_weight = centred(seeds[9], (MODEL_WIDTH, QUERY_WIDTH), MODEL_WIDTH ** -0.5, 0.0625, ((0, 2), (1, 8)))
    base_scale = jnp.clip(jnp.exp(math.log(2.0) - 1.3862944 * jax.random.uniform(seeds[10], (MODEL_WIDTH // GROUP, QUERY_WIDTH), jnp.float32) ** levels(seeds[10], (MODEL_WIDTH // GROUP, QUERY_WIDTH), ((0, 2), (1, 8)), -0.2, 0.2)), 0.5, 2.0).astype(jnp.bfloat16)
    row_hidden = centred(own_keys[11], (ROWS, MODEL_WIDTH), 1.0, 6.0, ((0, 8),))
    row_tenant = with_ends(skewed_ids(own_keys[12], (ROWS,), TENANT_COUNT, 2), jax.random.fold_in(own_keys[12], 3), 0, TENANT_COUNT - 1).astype(jnp.int32)
    cache_len = draw_cache_len(jax.random.fold_in(jax.random.fold_in(seeds[16], part), 71), part)
    kv_cache = draw_kv_cache(jax.random.fold_in(jax.random.fold_in(seeds[16], part), 71), part)
    new_kv = centred(own_keys[15], (ROWS, KV_HEADS, 2 * HEAD_DIM), 1.0, 6.0, ((0, 8), (1, 2)))
    return {"train_x": train_x, "train_cot": train_cot, "tenant_of_block": tenant_of_block, "down_factors": down_factors, "up_factors": up_factors, "down_mean_moment": down_mean_moment, "down_square_moment": down_square_moment, "up_mean_moment": up_mean_moment, "up_square_moment": up_square_moment, "base_weight": base_weight, "base_scale": base_scale, "row_hidden": row_hidden, "row_tenant": row_tenant, "cache_len": cache_len, "kv_cache": kv_cache, "new_kv": new_kv}


ADAPTER_SCALE = 2.0
FIRST_DECAY = 0.9
SECOND_DECAY = 0.999
FIRST_CORR = 1.0 / (1.0 - 0.9 ** 10)
SECOND_CORR = 1.0 / (1.0 - 0.999 ** 10)
ADAM_EPS = 1e-08
STEP_RATE = 0.002
TOP_PRECISION = lax.Precision.HIGHEST

def dequantize(base_weight, base_scale):
    spread = jnp.repeat(base_scale.astype(jnp.float32), GROUP, axis=0)
    return (base_weight.astype(jnp.float32) * spread).astype(jnp.bfloat16)

def moment_step_update(master, gradient, first, second):
    first_new = FIRST_DECAY * first + (1.0 - FIRST_DECAY) * gradient
    second_new = SECOND_DECAY * second + (1.0 - SECOND_DECAY) * gradient * gradient
    update = first_new * FIRST_CORR / (jnp.sqrt(second_new * SECOND_CORR) + ADAM_EPS)
    return (update, master - STEP_RATE * update)

def attend(query_vector, kv_cache, new_kv, cache_len):
    row_count = query_vector.shape[0]
    heads_kv = kv_cache.shape[1]
    grouped = query_vector.reshape(row_count, heads_kv, -1, HEAD_DIM).astype(jnp.float32)
    keys = kv_cache[..., :HEAD_DIM].astype(jnp.float32)
    values = kv_cache[..., HEAD_DIM:].astype(jnp.float32)
    inverse = 1.0 / math.sqrt(HEAD_DIM)
    scores = jnp.einsum('bkgh,bkph->bkgp', grouped, keys, precision=TOP_PRECISION) * inverse
    own_key = new_kv[..., :HEAD_DIM].astype(jnp.float32)
    own = jnp.einsum('bkgh,bkh->bkg', grouped, own_key, precision=TOP_PRECISION) * inverse
    live = (jnp.arange(CACHE, dtype=jnp.int32)[None, :] < cache_len[:, None])[:, None, None, :]
    top = jnp.maximum(lax.optimization_barrier(jnp.max(jnp.where(live, scores, -jnp.inf), axis=-1)), own)
    expo = jnp.where(live, jnp.exp(scores - top[..., None]), 0.0)
    own_expo = jnp.exp(own - top)
    total = lax.optimization_barrier(jnp.sum(expo, axis=-1)) + own_expo
    weights = (expo / total[..., None]).astype(jnp.bfloat16)
    own_weight = (own_expo / total).astype(jnp.bfloat16)
    own_value = new_kv[..., HEAD_DIM:].astype(jnp.float32)
    mixed = jnp.einsum('bkgp,bkph->bkgh', weights.astype(jnp.float32), values, precision=TOP_PRECISION)
    mixed = mixed + own_weight.astype(jnp.float32)[..., None] * own_value[:, :, None, :]
    return mixed.astype(jnp.bfloat16).reshape(row_count, -1)

def reference(train_x, train_cot, tenant_of_block, down_factors, up_factors, down_mean_moment, down_square_moment, up_mean_moment, up_square_moment, base_weight, base_scale, row_hidden, row_tenant, cache_len, kv_cache, new_kv):
    weight = dequantize(base_weight, base_scale)
    down_table = down_factors.astype(jnp.bfloat16).reshape(TENANT_COUNT, ADAPTER_RANK, MODEL_WIDTH)
    up_table = up_factors.astype(jnp.bfloat16).reshape(TENANT_COUNT, ADAPTER_RANK, QUERY_WIDTH)
    block_count = TRAIN_TOKENS // BLOCK
    input_blocks = train_x.reshape(block_count, BLOCK, MODEL_WIDTH)
    cotangent_blocks = train_cot.reshape(block_count, BLOCK, QUERY_WIDTH)

    def per_block_terms(items):
        x_block, cot_block, tenant = items
        tenant_down_rows = lax.dynamic_index_in_dim(down_table, tenant.astype(jnp.int32), 0, keepdims=False)
        up_rows = lax.dynamic_index_in_dim(up_table, tenant.astype(jnp.int32), 0, keepdims=False)
        u_low = jnp.dot(x_block, tenant_down_rows.T, preferred_element_type=jnp.float32).astype(jnp.bfloat16)
        gradient_lowrank = jnp.dot(cot_block, up_rows.T, preferred_element_type=jnp.float32).astype(jnp.bfloat16)
        down_gradient_piece = jnp.dot(gradient_lowrank.T, x_block, preferred_element_type=jnp.float32)
        up_gradient_piece = jnp.dot(u_low.T, cot_block, preferred_element_type=jnp.float32)
        adapter_piece = jnp.dot(gradient_lowrank, tenant_down_rows, preferred_element_type=jnp.float32)
        return (down_gradient_piece, up_gradient_piece, adapter_piece)
    down_gradient_blocks, up_gradient_blocks, adapter_input = lax.map(per_block_terms, (input_blocks, cotangent_blocks, tenant_of_block))
    tenant_ids = jnp.arange(TENANT_COUNT, dtype=jnp.int32)
    block_onehot = (tenant_of_block[:, None] == tenant_ids[None, :]).astype(jnp.float32)
    down_gradient = ADAPTER_SCALE * jnp.einsum('eg,eql->gql', block_onehot, down_gradient_blocks, precision=TOP_PRECISION).reshape(TENANT_COUNT * ADAPTER_RANK, MODEL_WIDTH)
    up_gradient = ADAPTER_SCALE * jnp.einsum('uv,uny->vny', block_onehot, up_gradient_blocks, precision=TOP_PRECISION).reshape(TENANT_COUNT * ADAPTER_RANK, QUERY_WIDTH)
    down_direction, revised_down = moment_step_update(down_factors, down_gradient, down_mean_moment, down_square_moment)
    up_direction, revised_up = moment_step_update(up_factors, up_gradient, up_mean_moment, up_square_moment)
    frozen_input_gradient = jnp.dot(train_cot, weight.T, preferred_element_type=jnp.float32)
    training_input_gradient = (frozen_input_gradient + ADAPTER_SCALE * adapter_input.reshape(TRAIN_TOKENS, MODEL_WIDTH)).astype(jnp.bfloat16)
    fresh_down = revised_down.astype(jnp.bfloat16).reshape(TENANT_COUNT, ADAPTER_RANK, MODEL_WIDTH).astype(jnp.float32)
    fresh_up = revised_up.astype(jnp.bfloat16).reshape(TENANT_COUNT, ADAPTER_RANK, QUERY_WIDTH).astype(jnp.float32)
    row_hot = (row_tenant[:, None] == tenant_ids[None, :]).astype(jnp.float32)
    row_down = jnp.einsum('bt,trd->brd', row_hot, fresh_down, precision=TOP_PRECISION)
    row_up = jnp.einsum('bt,trc->brc', row_hot, fresh_up, precision=TOP_PRECISION)
    row_u = jnp.einsum('bd,brd->br', row_hidden.astype(jnp.float32), row_down, precision=TOP_PRECISION).astype(jnp.bfloat16)
    adapter_difference = jnp.einsum('br,brc->bc', row_u.astype(jnp.float32), row_up, precision=TOP_PRECISION)
    frozen_query = jnp.dot(row_hidden, weight, preferred_element_type=jnp.float32)
    query_vector = (frozen_query + ADAPTER_SCALE * adapter_difference).astype(jnp.bfloat16)
    attended = attend(query_vector, kv_cache, new_kv, cache_len)
    return (down_direction, up_direction, training_input_gradient, attended)
```

```python
import functools
import math

import jax
import jax.numpy as jnp
from jax import lax
from jax.experimental import pallas as pl
from jax.experimental.pallas import tpu as pltpu
from jax.sharding import PartitionSpec as P

HEAD_DIM = 128
ADAPTER_RANK = 32
GROUP = 64
BLOCK = 128
CHUNKS = 4

ADAPTER_SCALE = 2.0
FIRST_DECAY = 0.9
SECOND_DECAY = 0.999
FIRST_CORR = 1.0 / (1.0 - 0.9**10)
SECOND_CORR = 1.0 / (1.0 - 0.999**10)
ADAM_EPS = 1e-08
STEP_RATE = 0.002
BF16 = jnp.bfloat16
F32 = jnp.float32
SMALL = pl.CostEstimate(flops=1024, bytes_accessed=1024, transcendentals=0)


def moment_step_update(master, gradient, first, second):
    first_new = FIRST_DECAY * first + (1.0 - FIRST_DECAY) * gradient
    second_new = SECOND_DECAY * second + (1.0 - SECOND_DECAY) * gradient * gradient
    update = first_new * FIRST_CORR / (jnp.sqrt(second_new * SECOND_CORR) + ADAM_EPS)
    return (update, master - STEP_RATE * update)


def attend(query_vector, kv_cache, new_kv, cache_len):
    row_count = query_vector.shape[0]
    heads_kv = kv_cache.shape[1]
    positions = kv_cache.shape[2]
    grouped = query_vector.reshape(row_count, heads_kv, -1, HEAD_DIM)
    keys = kv_cache[..., :HEAD_DIM]
    values = kv_cache[..., HEAD_DIM:]
    inverse = 1.0 / math.sqrt(HEAD_DIM)
    scores = jnp.einsum("bkgh,bkph->bkgp", grouped, keys, preferred_element_type=F32) * inverse
    own = (
        jnp.einsum("bkgh,bkh->bkg", grouped, new_kv[..., :HEAD_DIM], preferred_element_type=F32)
        * inverse
    )
    live = (jnp.arange(positions, dtype=jnp.int32)[None, :] < cache_len[:, None])[:, None, None, :]
    top = jnp.maximum(jnp.max(jnp.where(live, scores, -jnp.inf), axis=-1), own)
    expo = jnp.where(live, jnp.exp(scores - top[..., None]), 0.0)
    own_expo = jnp.exp(own - top)
    total = jnp.sum(expo, axis=-1) + own_expo
    weights = (expo / total[..., None]).astype(BF16)
    own_weight = (own_expo / total).astype(BF16)
    own_value = new_kv[..., HEAD_DIM:].astype(F32)
    mixed = jnp.einsum("bkgp,bkph->bkgh", weights, values, preferred_element_type=F32)
    mixed = mixed + own_weight.astype(F32)[..., None] * own_value[:, :, None, :]
    return mixed.astype(BF16).reshape(row_count, -1)


def bit_reversed(count):
    bits = count.bit_length() - 1
    return [int(format(i, "b").zfill(bits)[::-1], 2) if bits else 0 for i in range(count)]


def whole(shape):
    return pl.BlockSpec(shape, lambda *_: (0,) * len(shape))


def params(mib=40):
    return pltpu.CompilerParams(vmem_limit_bytes=mib * 2**20)


def pack(down, up, *more):
    parts = (down, up, *more)
    widths = [part.shape[1] for part in parts]

    def kernel(*refs):
        at = 0
        for ref, width in zip(refs, widths):
            refs[-1][:, at : at + width] = ref[...].astype(BF16)
            at += width

    return pl.pallas_call(
        kernel,
        out_shape=jax.ShapeDtypeStruct((down.shape[0], sum(widths)), BF16),
        compiler_params=params(),
        cost_estimate=SMALL,
    )(*parts)


def dequantize(base_weight, base_scale, y):
    rows, shard = base_weight.shape
    half = rows // CHUNKS // 2
    groups = half // GROUP
    scale = base_scale.reshape(2 * CHUNKS, groups, shard)

    def kernel(y_ref, weight_ref, scale_ref, out_ref, *pieces):
        spread = jnp.broadcast_to(
            scale_ref[0].astype(F32)[:, None, :], (groups, GROUP, shard)
        ).reshape(half, shard)
        value = (weight_ref[...].astype(F32) * spread).astype(BF16)
        out_ref[...] = value
        for k, piece in enumerate(pieces):

            @pl.when(pl.program_id(0) == 2 * k + y_ref[0])
            def _(piece=piece):
                piece[...] = value

    block = pl.BlockSpec((half, shard), lambda i, _: (i, 0))
    outs = pl.pallas_call(
        kernel,
        grid_spec=pltpu.PrefetchScalarGridSpec(
            num_scalar_prefetch=1,
            grid=(2 * CHUNKS,),
            in_specs=[block, pl.BlockSpec((1, groups, shard), lambda i, _: (i, 0, 0))],
            out_specs=[block] + [whole((half, shard))] * CHUNKS,
        ),
        out_shape=[jax.ShapeDtypeStruct((rows, shard), BF16)]
        + [jax.ShapeDtypeStruct((half, shard), BF16)] * CHUNKS,
        compiler_params=params(),
        cost_estimate=SMALL,
    )(y.reshape(1), base_weight, scale)
    return outs[0], outs[1:]


def shares_of(value, x):
    rows, columns = value.shape

    def kernel(x_ref, first_ref, second_ref, first_out, second_out):
        first_out[...] = first_ref[...]
        second_out[...] = second_ref[...]

    shape = (rows, columns // 2)
    return pl.pallas_call(
        kernel,
        grid_spec=pltpu.PrefetchScalarGridSpec(
            num_scalar_prefetch=1,
            grid=(1,),
            in_specs=[
                pl.BlockSpec(shape, lambda i, x: (0, x[0])),
                pl.BlockSpec(shape, lambda i, x: (0, x[0] ^ 1)),
            ],
            out_specs=[whole(shape)] * 2,
        ),
        out_shape=[jax.ShapeDtypeStruct(shape, value.dtype)] * 2,
        compiler_params=params(),
        cost_estimate=SMALL,
    )(x.reshape(1), value, value)


def arrange_kernel(shard, place, first_ref, second_ref, out_ref):
    x, near, core = place[0], place[1], place[2]
    for j in range(4):
        share, column = near ^ (j // 2), core ^ (j % 2)
        lanes = pl.ds(pl.multiple_of(column * shard, shard), shard)

        @pl.when(share == x)
        def _(j=j, lanes=lanes):
            out_ref[:, j * shard : (j + 1) * shard] = first_ref[:, lanes]

        @pl.when(share != x)
        def _(j=j, lanes=lanes):
            out_ref[:, j * shard : (j + 1) * shard] = second_ref[:, lanes]


def arrange(first, second, shard, place):
    rows, share = first.shape
    return pl.pallas_call(
        functools.partial(arrange_kernel, shard),
        grid_spec=pltpu.PrefetchScalarGridSpec(
            num_scalar_prefetch=1,
            grid=(1,),
            in_specs=[whole((rows, share))] * 2,
            out_specs=whole((rows, 2 * share)),
        ),
        out_shape=jax.ShapeDtypeStruct((rows, 2 * share), BF16),
        compiler_params=params(),
        cost_estimate=SMALL,
    )(place, first, second)


def project(parts, pick, x_in, cot, width, blocks):
    owned, total = parts[0].shape
    model = x_in.shape[1]
    count = len(parts)

    def kernel(pick_ref, x_ref, cot_ref, *refs):
        table_ref, low_ref, rest_ref, every = refs[count:]
        for i, ref in enumerate(refs[:count]):
            every[i * owned : (i + 1) * owned] = ref[:, :width]
            rest_ref[i * owned : (i + 1) * owned] = ref[:, width:]
        table_ref[...] = jnp.dot(
            pick_ref[...], every[...], preferred_element_type=F32
        ).astype(BF16)
        for b in range(blocks):
            tokens = slice(b * BLOCK, (b + 1) * BLOCK)
            ranks = slice(b * ADAPTER_RANK, (b + 1) * ADAPTER_RANK)
            low_ref[tokens, :ADAPTER_RANK] = lax.dot_general(
                x_ref[tokens],
                table_ref[ranks, :model],
                (((1,), (1,)), ((), ())),
                preferred_element_type=F32,
            )
            low_ref[tokens, ADAPTER_RANK:] = lax.dot_general(
                cot_ref[tokens],
                table_ref[ranks, model:],
                (((1,), (1,)), ((), ())),
                preferred_element_type=F32,
            )

    return pl.pallas_call(
        kernel,
        out_shape=[
            jax.ShapeDtypeStruct((blocks * ADAPTER_RANK, width), BF16),
            jax.ShapeDtypeStruct((x_in.shape[0], 2 * ADAPTER_RANK), F32),
            jax.ShapeDtypeStruct((count * owned, total - width), BF16),
        ],
        scratch_shapes=[pltpu.VMEM((count * owned, width), BF16)],
        compiler_params=params(),
        cost_estimate=SMALL,
    )(pick, x_in, cot, *parts)


def factor_gradients(low, rank_of, belongs, x_in, cot):
    slots = rank_of.shape[1]
    half = slots // 2
    model, width = x_in.shape[1], x_in.shape[1] + cot.shape[1]

    def kernel(low_ref, rank_ref, belongs_ref, x_ref, cot_ref, keep_ref, send_ref):
        for at, source, ranks in (
            (0, x_ref, slice(ADAPTER_RANK, 2 * ADAPTER_RANK)),
            (model, cot_ref, slice(0, ADAPTER_RANK)),
        ):
            wide = jnp.dot(low_ref[:, ranks], rank_ref[...], preferred_element_type=F32)
            wide = (wide * belongs_ref[...]).astype(BF16)
            columns = source.shape[1]
            for first in range(0, columns, 512):
                size = min(512, columns - first)
                product = lax.dot_general(
                    wide,
                    source[:, first : first + size],
                    (((0,), (0,)), ((), ())),
                    preferred_element_type=F32,
                )
                lanes = slice(at + first, at + first + size)
                keep_ref[:, lanes] = product[:half]
                send_ref[:, lanes] = product[half:].astype(BF16)

    return pl.pallas_call(
        kernel,
        out_shape=[
            jax.ShapeDtypeStruct((half, width), F32),
            jax.ShapeDtypeStruct((half, width), BF16),
        ],
        compiler_params=params(),
        cost_estimate=SMALL,
    )(low, rank_of, belongs, x_in, cot)


def through_weight(cot, weight, weight_core, near, chunk, y, adapter=None):
    tokens = cot.shape[0]
    half, shard = near[0].shape
    rows = 2 * half

    def kernel(y_ref, cot_ref, own_ref, core_ref, mine, other, mine_core, other_core, *refs):
        out_ref = refs[-1]

        def run(near_ref, near_core_ref):
            total = None
            for j, ref in enumerate((own_ref, core_ref, near_ref, near_core_ref)):
                term = lax.dot_general(
                    cot_ref[:, j * shard : (j + 1) * shard],
                    ref[...],
                    (((1,), (1,)), ((), ())),
                    preferred_element_type=F32,
                )
                total = term if total is None else total + term
            if adapter is not None:
                total = total + ADAPTER_SCALE * jnp.dot(
                    refs[0][...], refs[1][...], preferred_element_type=F32
                )
            out_ref[...] = total.astype(out_ref.dtype)

        @pl.when(pl.program_id(0) == y_ref[0])
        def _():
            run(mine, mine_core)

        @pl.when(pl.program_id(0) != y_ref[0])
        def _():
            run(other, other_core)

    block = pl.BlockSpec((half, shard), lambda i, _: (2 * chunk + i, 0))
    operands = [cot, weight, weight_core, *near]
    specs = [whole(cot.shape), block, block] + [whole((half, shard))] * 4
    if adapter is not None:
        low, table = adapter
        operands += [low, table]
        specs += [
            whole(low.shape),
            pl.BlockSpec((table.shape[0], half), lambda i, _: (0, 2 * chunk + i)),
        ]
    dtype = BF16 if adapter is None else F32
    return pl.pallas_call(
        kernel,
        grid_spec=pltpu.PrefetchScalarGridSpec(
            num_scalar_prefetch=1,
            grid=(2,),
            in_specs=specs,
            out_specs=pl.BlockSpec((tokens, half), lambda i, _: (0, i)),
        ),
        out_shape=jax.ShapeDtypeStruct((tokens, rows), dtype),
        compiler_params=params(),
        cost_estimate=SMALL,
    )(y.reshape(1), *operands)


def final_kernel(count, own_ref, *refs):
    away, out_ref = refs[:count], refs[-1]
    total = own_ref[...]
    for part in away:
        total = total + part[...].astype(F32)
    out_ref[...] = total.astype(BF16)


def finish(own, away, out, chunk, model):
    tokens, rows = own.shape
    operands = [own, *away]
    specs = [whole(own.shape)] + [whole(part.shape) for part in away]
    aliases = {}
    if out is not None:
        aliases = {len(operands): 0}
        operands.append(out)
        specs.append(pl.BlockSpec(memory_space=pl.ANY))
    return pl.pallas_call(
        functools.partial(final_kernel, len(away)),
        grid=(1,),
        in_specs=specs,
        out_specs=pl.BlockSpec((tokens, rows), lambda i: (0, chunk)),
        out_shape=jax.ShapeDtypeStruct((tokens, model), BF16),
        input_output_aliases=aliases,
        compiler_params=params(),
        cost_estimate=SMALL,
    )(*operands)


def local(sizes, *arguments):
    (
        train_x,
        train_cot,
        tenant_of_block,
        down_factors,
        up_factors,
        down_mean_moment,
        down_square_moment,
        up_mean_moment,
        up_square_moment,
        base_weight,
        base_scale,
        row_hidden,
        row_tenant,
        cache_len,
        kv_cache,
        new_kv,
    ) = arguments
    depth, cores, halves = sizes["dp"], sizes["role"], sizes["mp"]
    y, z = lax.axis_index("groups"), lax.axis_index("dp")
    x, core = lax.axis_index("mp"), lax.axis_index("role")
    token_rows, model_local = train_x.shape
    query_local = train_cot.shape[1]
    block_count = token_rows // BLOCK
    owned = down_factors.shape[0]
    shard = base_weight.shape[1]
    order = bit_reversed(depth)

    def swap(value, axis, mask=1):
        return lax.ppermute(value, axis, [(i, i ^ mask) for i in range(sizes[axis])])

    def total_mp(value):
        mask = 1
        while mask < halves:
            value = value + swap(value, "mp", mask)
            mask *= 2
        return value

    def after(value, *others):
        return lax.optimization_barrier((value, others))[0]

    last = [None]

    def joint(*values):
        behind = () if last[0] is None else (last[0],)
        out = lax.optimization_barrier((*values, *behind))[: len(values)]
        last[0] = out[0]
        return out

    def mark(value):
        last[0] = value
        return value

    rows_own = row_hidden.shape[0]
    hidden_width = rows_own * model_local // owned
    hidden_own = lax.dynamic_slice_in_dim(row_hidden, x * model_local, model_local, 1)
    factors = pack(
        down_factors,
        up_factors,
        hidden_own.reshape(owned, hidden_width),
        jnp.broadcast_to(
            jnp.pad(row_tenant.astype(BF16), (0, 128 - rows_own))[None, :], (owned, 128)
        ),
    )
    far = swap(factors, "dp", depth // 2)
    early = swap(factors, "dp", depth // 4)
    held = {0: factors, depth // 2: far}
    first, second = shares_of(train_cot, x) if halves == 2 else (factors, factors)
    mines, others = [None] * CHUNKS, [None] * CHUNKS

    assert depth == 2 * halves and query_local == 2 * cores * shard
    pair = z // 2
    away_masks = list(range(2, depth, 2))

    def wide_cotangents():
        every = lax.all_gather(train_cot, "mp", axis=1, tiled=True)

        def columns(value, base):
            return jnp.concatenate(
                [
                    lax.dynamic_slice_in_dim(value, (zz * cores + cc) * shard - base, shard, 1)
                    for zz in (z, z ^ 1)
                    for cc in (core, core ^ 1)
                ],
                axis=1,
            )

        found = [columns(every, 0)]
        for mask in away_masks:
            wanted = (pair ^ (mask // 2)) * query_local
            got = swap(lax.dynamic_slice_in_dim(every, wanted, query_local, 1), "dp", mask)
            found.append(columns(got, pair * query_local))
        return found

    mask = depth // 4
    if halves == 2:
        near_first = swap(second, "mp")
        weight, pieces = dequantize(after(base_weight, near_first), base_scale, y)
        far, near_first, early, weight = joint(far, near_first, early, weight)
        far_cot = swap(jnp.where(x == pair, near_first, first), "dp", 2)
    else:
        cot_own, *cot_away = wide_cotangents()
        weight, pieces = dequantize(base_weight, base_scale, y)
        far, early, weight = joint(far, early, weight)
        far_cot = far

    weight_core = swap(weight, "role")
    mines[0] = swap(pieces[0], "dp", 1)

    held[depth // 2] = far
    while mask:
        for slot in list(held):
            given = mask == depth // 4 and slot == 0
            held[slot ^ mask] = early if given else swap(held[slot], "dp", mask)
        mask //= 2
    zl = after(z, far)
    tenants = after(tenant_of_block, far)
    slots = jnp.array(order, jnp.int32)
    owners = jnp.concatenate([(zl ^ slots) * cores + core, (zl ^ slots) * cores + (core ^ 1)])
    row_ids = (owners[:, None] * owned + jnp.arange(owned, dtype=jnp.int32)[None, :]).reshape(-1)
    wanted = tenants[:, None] * ADAPTER_RANK + jnp.arange(ADAPTER_RANK, dtype=jnp.int32)
    pick = (wanted.reshape(-1)[:, None] == row_ids[None, :]).astype(BF16)
    rank_of = (
        jnp.arange(ADAPTER_RANK, dtype=jnp.int32)[:, None] == (row_ids % ADAPTER_RANK)[None, :]
    ).astype(BF16)
    token_tenant = jnp.repeat(tenants, BLOCK)
    belongs = (token_tenant[:, None] == (row_ids // ADAPTER_RANK)[None, :]).astype(F32)

    mine = [held[slot] for slot in order]
    mine_cores, other_cores = [None] * CHUNKS, [None] * CHUNKS

    def fetch(k):
        mines[k] = swap(after(pieces[k], last[0]), "dp", 1)

    def to_core(value, *behind):
        return swap(after(value, *behind) if behind else value, "role")

    width = model_local + query_local
    count = len(mine)
    own_near = swap(mine[0], "role")
    far_cot, mines[0], weight_core, own_near, *found = joint(
        far_cot, mines[0], weight_core, own_near, *mine
    )
    far_cot_near = swap(far_cot, "mp") if halves == 2 else far_cot
    others[0] = swap(mines[0], "groups")
    fetch(1)
    parts = joint(*found, own_near, *[swap(part, "role") for part in found[1:]])
    table, low_terms, beside = project(parts, pick, train_x, train_cot, width, block_count)
    low_sum = total_mp(mark(low_terms))
    hidden = beside[:, :hidden_width].reshape(-1, model_local)
    hidden_tenant = beside[:, hidden_width:].reshape(-1, owned, 128)[:, 0, :rows_own]
    hidden_tenant = hidden_tenant.reshape(-1)

    low_sum, mine_cores[0], other_cores[0], mine_cores[1] = joint(
        low_sum,
        to_core(mines[0], far_cot_near, low_terms),
        to_core(others[0], low_terms),
        to_core(mines[1], low_terms),
    )
    fetch(2)
    low = low_sum.astype(BF16)
    keep, give = factor_gradients(low, rank_of, belongs, train_x, train_cot)
    got = swap(mark(give), "role")
    if halves == 2:
        place = jnp.stack([x, z % 2, core])
        cot_away = [mark(arrange(far_cot, after(far_cot_near, give), shard, place))]

    sent, arrived = [None] * CHUNKS, [None] * CHUNKS

    def partial(k, behind):
        near = (mines[k], others[k], mine_cores[k], other_cores[k])
        sent[k] = [
            through_weight(after(cot, behind), weight, weight_core, near, k, y)
            for cot in cot_away
        ]

    def send(k):
        arrived[k] = [swap(value, "dp", mask) for value, mask in zip(sent[k], away_masks)]

    def echo(value):
        return swap(value[:16, :128], "role")

    def stage(value, axis, mask, dtype):
        half = value.shape[0] // 2
        sent = mark(value[half:].astype(dtype))
        return value[:half], swap(sent, axis, mask)

    def settle(kept, got):
        return kept.astype(F32) + after(got, last[0]).astype(F32)

    masks = [1 << i for i in range(depth.bit_length() - 1)]
    partial(0, give)
    send(0)
    got, mines[2], *sent[0] = joint(got, mines[2], *sent[0])
    others[1] = swap(mines[1], "groups")
    kept, got = stage(settle(keep, got), "dp", masks[0], BF16)
    other_cores[1] = to_core(others[1])
    partial(1, give)
    send(1)
    far_second = swap(after(first, give), "mp") if halves == 2 else got
    mine_cores[2] = to_core(
        mines[2], got, echo(arrived[0][0]), far_second, sent[1][0]
    )
    got, mine_cores[2], far_second, *rest = joint(
        got, mine_cores[2], far_second, *arrived[0], *sent[1]
    )
    arrived[0] = rest[: len(sent[1])]
    others[2] = swap(mines[2], "groups")
    fetch(3)
    for mask in masks[1:]:
        kept, got = stage(settle(kept, got), "dp", mask, BF16)
    other_cores[2] = to_core(others[2])
    partial(2, got if depth > 4 else give)
    send(2)
    base_query = jnp.dot(after(hidden, sent[1][0]), weight, preferred_element_type=F32)
    mine_cores[3] = to_core(
        mines[3], got, echo(arrived[1][0]), sent[2][0], base_query
    )
    got, mine_cores[3], base_query, *rest = joint(
        got, mine_cores[3], base_query, *arrived[1], *sent[2]
    )
    arrived[1] = rest[: len(sent[2])]
    others[3] = swap(mines[3], "groups")
    other_cores[3] = to_core(others[3])
    partial(3, mine_cores[3])

    gradient = settle(kept, got)
    down_direction, revised_down = moment_step_update(
        down_factors,
        ADAPTER_SCALE * gradient[:, :model_local],
        down_mean_moment,
        down_square_moment,
    )
    up_direction, revised_up = moment_step_update(
        up_factors, ADAPTER_SCALE * gradient[:, model_local:], up_mean_moment, up_square_moment
    )
    fresh_down, fresh_up = revised_down.astype(BF16), revised_up.astype(BF16)

    rank_terms = lax.dot_general(
        hidden, fresh_down, (((1,), (1,)), ((), ())), preferred_element_type=F32
    )
    both = total_mp(
        jnp.concatenate(
            [base_query, jnp.pad(rank_terms, ((0, 0), (0, -rank_terms.shape[1] % 128)))], axis=1
        )
    )
    base_query, rank_terms = both[:, :shard], both[:, shard : shard + owned]
    first_col = (z * cores + core) * shard
    placed = lax.dynamic_update_slice(
        jnp.zeros((hidden.shape[0], query_local), F32),
        base_query,
        (0, first_col % query_local),
    )
    placed = jnp.where(x == first_col // query_local, placed, 0.0)
    my_tenant = ((z * cores + core) * owned + jnp.arange(owned, dtype=jnp.int32)) // ADAPTER_RANK
    row_low = jnp.where(
        hidden_tenant.astype(jnp.int32)[:, None] == my_tenant[None, :], rank_terms, 0.0
    ).astype(BF16)
    delta = jnp.dot(row_low, fresh_up, preferred_element_type=F32)
    query = placed + ADAPTER_SCALE * delta
    half = query.shape[0] // 2
    kept, got = query[:half], swap(after(query[half:], echo(arrived[2][0]), sent[3][0]), "role")
    got, *rest = joint(got, *arrived[2], *sent[3])
    arrived[2], sent[3] = rest[: len(sent[3])], rest[len(sent[3]) :]
    send(3)
    for mask in masks:
        kept, got = stage(settle(kept, got), "dp", mask, F32)

    block_of = jnp.repeat(jnp.arange(block_count, dtype=jnp.int32), BLOCK)
    col_block = jnp.repeat(jnp.arange(block_count, dtype=jnp.int32), ADAPTER_RANK)
    low_blocks = jnp.where(
        block_of[:, None] == col_block[None, :],
        jnp.tile(low[:, ADAPTER_RANK:], (1, block_count)),
        0,
    ).astype(BF16)
    if halves == 2:
        cot_own = arrange(
            jnp.where(x == pair, first, near_first),
            jnp.where(x == pair, second, far_second),
            shard,
            place,
        )
    owns = []
    for k in range(CHUNKS):
        near = (mines[k], others[k], mine_cores[k], other_cores[k])
        owns.append(
            through_weight(cot_own, weight, weight_core, near, k, y, adapter=(low_blocks, table))
        )
    out = None
    for k in range(CHUNKS - 1):
        out = finish(owns[k], arrived[k], out, k, model_local)
    got, out, owns[-1], *arrived[-1] = joint(got, out, owns[-1], *arrived[-1])
    out = finish(owns[-1], arrived[-1], out, CHUNKS - 1, model_local)
    query = settle(kept, got).astype(BF16)
    attended = attend(query, kv_cache, new_kv, cache_len)
    return (down_direction, up_direction, out, attended)


def solution(mesh):
    rows = ("groups", "dp", "role")
    in_specs = (
        P(rows, "mp"),
        P(rows, "mp"),
        P(rows),
        P(rows, "mp"),
        P(rows, "mp"),
        P(rows, "mp"),
        P(rows, "mp"),
        P(rows, "mp"),
        P(rows, "mp"),
        P("mp", ("dp", "role")),
        P("mp", ("dp", "role")),
        P(rows, None),
        P(rows),
        P(rows),
        P(rows, "mp", None, None),
        P(rows, "mp", None),
    )
    out_specs = (P(rows, "mp"), P(rows, "mp"), P(rows, "mp"), P(rows, "mp"))
    sizes = dict(mesh.shape)
    return jax.shard_map(
        functools.partial(local, sizes),
        mesh=mesh,
        in_specs=in_specs,
        out_specs=out_specs,
        check_vma=False,
    )
```
